32 devices in a mesh: rep: 2 (over y), grp: 4 (over z), ing: 2 (over x), dp: 2 (over core).
Axes of the slice: x: 2, y: 2, z: 4, core: 2. Of those that a mesh axis runs over, the one named last changes fastest.
Arguments:
- tokens: bfloat16 [8192, 7168], P(('rep', 'grp', 'ing', 'dp')), parts along dimension 0, may hold values from -6 to 6
- routes: int32 [8192, 8], P(('rep', 'grp', 'ing', 'dp')), parts along dimension 0, may hold values from 0 to 255, as said below
- route_gates: float32 [8192, 8], P(('rep', 'grp', 'ing', 'dp')), parts along dimension 0, may hold values from 0.2 to 2.5
- gate_proj: bfloat16 [4, 7168, 1024], P('grp', None, ('ing', 'dp')), may hold values from -0.0625 to 0.0625
- up_proj: bfloat16 [4, 7168, 1024], P('grp', None, ('ing', 'dp')), may hold values from -0.0625 to 0.0625
- down_proj: bfloat16 [4, 1024, 7168], P('grp', ('ing', 'dp')), may hold values from -0.1875 to 0.1875
Outputs:
- moe_out: bfloat16 [8192, 7168], P(('rep', 'grp', 'ing', 'dp')), parts along dimension 0
The draws below stay inside these ranges and needn't reach their ends.
There are 2 independent parts, one for each index of `rep`. The reference program is written for one: setup_inputs(seed, part) draws one part's arguments, and reference() takes and returns one part's arrays. A program takes and returns all parts, laid end to end along the dimension named above; an argument that names none is the same for every part. Nothing has to cross between parts.
Inputs may be any that keep to these rules, and one draw needn't show every extreme that they name: `routes`: the 8 ids of a token are distinct and at most one of them is a multiple of 64. Within the rows of one device no multiple of 64 stands in more than 32 rows, and one such id stands in exactly 32 rows of every device.
All inputs are finite; a program needn't handle non-finite values.
Results may differ from the reference program's by a relative error of at most 0.011.
Values may be sent and summed in bfloat16 or wider, within the bound.
A program may use at most 128 MiB of HBM per device.

```python
import jax
import jax.numpy as jnp
from jax import lax

D = 7168
FF = 1024
EXPERTS = 256
TOPK = 8
TOK_DEV = 256
TOKENS = 4096
EXP_WIN = 4
STRIDE = 64
CAP = 32
N_GRP = 4
N_ING = 2
N_DP = 2


def draw_routes(key, part):
    key = jax.random.fold_in(key, 11)
    key_level, key_count, key_hot, key_order, key_slot, key_offset, key_group = jax.random.split(key, 7)
    block_count = TOKENS // TOK_DEV
    levels = jax.random.randint(key_level, (N_GRP,), 2, 5)
    ceiling = levels * CAP // 4
    counts = jax.random.randint(key_count, (block_count, N_GRP), 0, ceiling[None, :] + 1)
    hot_expert = jax.random.randint(key_hot, (), 0, N_GRP)
    counts = jnp.where(jnp.arange(N_GRP)[None, :] == hot_expert, CAP, counts)
    upper = jnp.cumsum(counts, axis=1)
    lower = upper - counts
    ordering = jax.vmap(lambda sub_key: jax.random.permutation(sub_key, TOK_DEV))(jax.random.split(key_order, block_count))
    position = ordering[:, :, None]
    inside = (position >= lower[:, None, :]) & (position < upper[:, None, :])
    landed = jnp.any(inside, axis=2)
    owners = jnp.sum(inside.astype(jnp.int32) * jnp.arange(N_GRP)[None, None, :], axis=2)
    window_ids = owners * STRIDE
    slot_index = jnp.arange(TOPK)
    first_group = jax.random.randint(key_group, (block_count, TOK_DEV, 1), 0, 8)
    group_ids = (first_group + slot_index[None, None, :] // 2) % 8
    offsets = jax.random.randint(key_offset, (block_count, TOK_DEV, TOPK), 1, 8) + 8 * (slot_index % 2)[None, None, :]
    expert_ids = group_ids * (EXPERTS // 8) + offsets
    hit_slot = jax.random.randint(key_slot, (block_count, TOK_DEV, 1), 0, TOPK)
    expert_ids = jnp.where(landed[:, :, None] & (slot_index[None, None, :] == hit_slot), window_ids[:, :, None], expert_ids)
    return expert_ids.reshape(TOKENS, TOPK).astype(jnp.int32)


def steps_of(rng, shape, cuts, smallest, high):
    def one(dim, shards_of):
        heights = jax.random.uniform(jax.random.fold_in(jax.random.fold_in(rng, 6), dim), (shards_of,), jnp.float32, smallest / len(cuts), high / len(cuts))
        return jnp.repeat(jnp.exp(heights), shape[dim] // shards_of).reshape((-1,) + (1,) * (len(shape) - dim - 1))

    gain = one(*cuts[0])
    for cut in cuts[1:]:
        gain = gain * one(*cut)
    return gain


def noise(stream_key, extent, spread, most, cuts=(), kind=jnp.bfloat16):
    loudness = steps_of(stream_key, extent, cuts, -0.22, 0.18) if cuts else 1.0
    array = jax.random.normal(stream_key, extent, jnp.float32) * spread * loudness
    return jnp.minimum(jnp.maximum(array, -most), most).astype(kind)


def setup_inputs(seed: int = 0, part: int = 0) -> dict:
    key_list = jax.random.split(jax.random.key(seed), 7)
    part_splits = jax.random.split(jax.random.fold_in(key_list[6], part), 7)
    return {
        "tokens": noise(part_splits[0], (TOKENS, D), 1.0, 6.0, ((0, 16),)),
        "routes": draw_routes(jax.random.fold_in(jax.random.fold_in(key_list[6], part), 71), part),
        "route_gates": jnp.clip(0.2 + 2.3 * jax.random.uniform(part_splits[2], (TOKENS, TOPK), jnp.float32) ** steps_of(part_splits[2], (TOKENS, TOPK), ((0, 16),), -0.2, 0.2), 0.2, 2.5),
        "gate_proj": noise(key_list[3], (EXP_WIN, D, FF), D ** -0.5, 0.0625, ((0, 4), (2, 4))),
        "up_proj": noise(key_list[4], (EXP_WIN, D, FF), D ** -0.5, 0.0625, ((0, 4), (2, 4))),
        "down_proj": noise(key_list[5], (EXP_WIN, FF, D), FF ** -0.5, 0.1875, ((0, 4), (1, 4))),
    }


def reference(tokens, routes, route_gates, gate_proj, up_proj, down_proj):
    struck = (routes % STRIDE) == 0
    gate_sum = jnp.sum(jnp.where(struck, route_gates, jnp.zeros_like(route_gates)), axis=1)
    max_rows = CAP * N_GRP * N_ING * N_DP
    block_count = N_ING
    block_size = FF // block_count

    def one_expert(routed_sum, expert):
        chosen = jnp.any(routes == expert * STRIDE, axis=1)
        picked = jnp.nonzero(chosen, size=max_rows, fill_value=0)[0].astype(jnp.int32)
        filled = jnp.arange(max_rows, dtype=jnp.int32) < jnp.sum(chosen.astype(jnp.int32))
        routed_rows = tokens[picked]
        gate_act = jnp.dot(routed_rows, gate_proj[expert], preferred_element_type=jnp.float32)
        up_act = jnp.dot(routed_rows, up_proj[expert], preferred_element_type=jnp.float32)
        hidden = (jax.nn.silu(gate_act) * up_act).astype(jnp.bfloat16)
        hidden_blocks = hidden.reshape(max_rows, block_count, block_size).astype(jnp.float32)
        down_blocks = down_proj[expert].reshape(block_count, block_size, D).astype(jnp.float32)
        block_parts = jnp.einsum("rbf,bfd->rbd", hidden_blocks, down_blocks).astype(jnp.bfloat16)
        row_out = jnp.sum(block_parts.astype(jnp.float32), axis=1).astype(jnp.bfloat16)
        contrib = jnp.where(filled[:, None], row_out.astype(jnp.float32), jnp.zeros((max_rows, D), jnp.float32))
        return routed_sum.at[picked].add(contrib), None

    routed, _ = lax.scan(one_expert, jnp.zeros((TOKENS, D), jnp.float32), jnp.arange(EXP_WIN, dtype=jnp.int32))
    return (gate_sum[:, None] * routed).astype(jnp.bfloat16)
```

```python
import functools

import jax
import jax.numpy as jnp
from jax import lax
from jax.experimental import pallas as pl
from jax.experimental.pallas import tpu as pltpu
from jax.sharding import PartitionSpec as P

EXPERTS = 256
MESH = pl.DeviceIdType.MESH


def expert_rows(routed_rows, weight_set):
    gate_weight, up_weight, down_weight = weight_set
    gathered = lax.all_gather(routed_rows, "ing", axis=0, tiled=True)
    gate_act = jnp.dot(gathered, gate_weight[0], preferred_element_type=jnp.float32)
    up_act = jnp.dot(gathered, up_weight[0], preferred_element_type=jnp.float32)
    hidden = (jax.nn.silu(gate_act) * up_act).astype(jnp.bfloat16)
    return lax.psum_scatter(
        jnp.dot(hidden, down_weight[0], preferred_element_type=jnp.float32).astype(jnp.bfloat16),
        "ing",
        scatter_dimension=0,
        tiled=True,
    )


def swapped(z, d):
    flipped = z
    if d % 2:
        flipped = flipped + 1 - 2 * (z % 2)
    if d // 2:
        flipped = flipped + 2 - 4 * ((z // 2) % 2)
    return flipped


def expert_kernel(
    outgoing, gate_hbm, up_hbm, down_hbm, returned,
    gate_w, up_w, down_w, rows, kept, leaving, coming, summed,
    local_sem, weight_send, weight_recv, zin_send, zin_recv, xin_send, xin_recv,
    xout_send, xout_recv, zout_send, zout_recv,
):
    z, x, c = (lax.axis_index(name) for name in ("grp", "ing", "dp"))
    across, sibling = {"ing": 1 - x}, {"dp": 1 - c}
    half_rows, width = rows.shape[3], rows.shape[4]

    barrier = pltpu.get_barrier_semaphore()
    peers = [across, sibling] + [{"grp": swapped(z, d)} for d in (1, 2, 3)]
    for peer in peers:
        pl.semaphore_signal(barrier, inc=1, device_id=peer, device_id_type=MESH)
    pl.semaphore_wait(barrier, len(peers))

    def remote(src, dst, send, recv, to):
        return pltpu.make_async_remote_copy(
            src_ref=src, dst_ref=dst, send_sem=send, recv_sem=recv, device_id=to, device_id_type=MESH
        )

    def zin(d, h):
        t = swapped(z, d)
        return remote(outgoing.at[t, h], rows.at[d, h, 0], zin_send.at[d, h], zin_recv.at[d, h], {"grp": t})

    def xin(d, h):
        return remote(rows.at[d, h, 0], rows.at[d, h, 1], xin_send.at[d, h], xin_recv.at[d, h], across)

    def xout(d, h):
        return remote(leaving.at[d, h], coming.at[d, h], xout_send.at[d, h], xout_recv.at[d, h], across)

    def zout(d, h, t):
        return remote(summed.at[d, h], returned.at[z, h], zout_send.at[d, h], zout_recv.at[d, h], {"grp": t})

    def flipped(d):
        low, high = d % 2, d // 2
        return z + low * (1 - 2 * (z % 2)) + high * (2 - 4 * ((z // 2) % 2))

    for h in range(2):
        zin(2, h).start()
    for h in range(2):
        rows[0, h, 0] = outgoing[z, h]
        xin(0, h).start()
    for h in range(2):
        zin(1, h).start()
    weights = []
    for i, (hbm, vmem) in enumerate(((gate_hbm, gate_w), (up_hbm, up_w), (down_hbm, down_w))):
        own = pltpu.make_async_copy(hbm, vmem.at[0], local_sem.at[i])
        other = remote(hbm, vmem.at[1], weight_send.at[i], weight_recv.at[i], sibling)
        own.start()
        other.start()
        weights.append((own, other))
    for h in range(2):
        zin(2, h).wait_recv()
        xin(2, h).start()
        zin(3, h).start()
    for h in range(2):
        zin(1, h).wait_recv()
        xin(1, h).start()
    for own, other in weights[:2]:
        own.wait()
        other.wait_recv()

    def chunk_of(i):
        pair = i // 2
        return 2 * (1 - pair % 2) + pair // 2, i % 2

    def finish(i):
        d, h = chunk_of(i)
        xout(d, h).wait_recv()
        summed[d, h] = (kept[d, h] + coming[d, h].astype(jnp.float32)).astype(jnp.bfloat16)

        @pl.when(d == 0)
        def _():
            pltpu.make_async_copy(summed.at[d, h], returned.at[z, h], local_sem.at[3 + h]).start()

        @pl.when(d != 0)
        def _():
            zout(d, h, flipped(d)).start()

    def compute(i, carry):
        d, h = chunk_of(i)
        xin(d, h).wait_recv()
        chunk = rows.at[d, h]
        tile = chunk[...].reshape(2 * half_rows, width)
        hidden = []
        for w in range(2):
            gate_act = jnp.dot(tile, gate_w[w], preferred_element_type=jnp.float32)
            up_act = jnp.dot(tile, up_w[w], preferred_element_type=jnp.float32)
            hidden.append((gate_act / (1.0 + jnp.exp(-gate_act)) * up_act).astype(jnp.bfloat16))

        @pl.when(i == 0)
        def _():
            weights[2][0].wait()
            weights[2][1].wait_recv()

        step = 1024

        def down(n, carry):
            columns = pl.ds(pl.multiple_of(n * step, step), step)
            part = jnp.dot(hidden[0], down_w[0, :, columns], preferred_element_type=jnp.float32)
            part += jnp.dot(hidden[1], down_w[1, :, columns], preferred_element_type=jnp.float32)
            kept[d, h, :, columns] = part[:half_rows]
            leaving[d, h, :, columns] = part[half_rows:].astype(jnp.bfloat16)
            return carry

        lax.fori_loop(0, width // step, down, 0)
        xout(d, h).start()

        @pl.when((i == 1) | (i == 3))
        def _():
            zin(3, i // 2).wait_recv()
            xin(3, i // 2).start()

        @pl.when(i >= 2)
        def _():
            finish(i - 2)

        return carry

    lax.fori_loop(0, 8, compute, 0)
    for i in (6, 7):
        finish(i)
    for own, other in weights:
        other.wait_send()
    for h in range(2):
        pltpu.make_async_copy(summed.at[0, h], returned.at[z, h], local_sem.at[3 + h]).wait()
        for d in range(4):
            xin(d, h).wait_send()
            xout(d, h).wait_send()
            if d:
                zin(d, h).wait_send()
                zout(d, h, swapped(z, d)).wait()


def expert_call(outgoing, gate_proj, up_proj, down_proj):
    groups, slot_count, model_width = outgoing.shape
    hidden = gate_proj.shape[2]
    halves = (groups, 2, slot_count // 2, model_width)
    dma = pltpu.SemaphoreType.DMA
    vmem, hbm = pl.BlockSpec(memory_space=pltpu.VMEM), pl.BlockSpec(memory_space=pl.ANY)
    bf16, f32 = jnp.bfloat16, jnp.float32
    returned = pl.pallas_call(
        expert_kernel,
        out_shape=jax.ShapeDtypeStruct(halves, bf16),
        in_specs=[vmem, hbm, hbm, hbm],
        out_specs=hbm,
        scratch_shapes=[
            pltpu.VMEM((2, model_width, hidden), bf16),
            pltpu.VMEM((2, model_width, hidden), bf16),
            pltpu.VMEM((2, hidden, model_width), bf16),
            pltpu.VMEM((groups, 2, 2, slot_count // 2, model_width), bf16),
            pltpu.VMEM(halves, f32),
            pltpu.VMEM(halves, bf16),
            pltpu.VMEM(halves, bf16),
            pltpu.VMEM(halves, bf16),
            dma((5,)),
            dma((3,)),
            dma((3,)),
        ]
        + [dma((groups, 2))] * 8,
        compiler_params=pltpu.CompilerParams(
            collective_id=0, has_side_effects=True, vmem_limit_bytes=56 * 2**20
        ),
        name="routed_experts",
    )(outgoing.reshape(halves), gate_proj[0], up_proj[0], down_proj[0])
    return returned.reshape(groups, slot_count, model_width)


def plain_call(outgoing, gate_proj, up_proj, down_proj):
    groups, slot_count, model_width = outgoing.shape
    arrived = lax.all_to_all(outgoing, "grp", split_axis=0, concat_axis=0, tiled=True)
    weight_set = (
        lax.all_gather(gate_proj, "dp", axis=2, tiled=True),
        lax.all_gather(up_proj, "dp", axis=2, tiled=True),
        lax.all_gather(down_proj, "dp", axis=1, tiled=True),
    )
    results = expert_rows(arrived.reshape(-1, model_width), weight_set).reshape(
        groups, slot_count, model_width
    )
    return lax.all_to_all(results, "grp", split_axis=0, concat_axis=0, tiled=True)


def on_device(tokens, routes, route_gates, gate_proj, up_proj, down_proj):
    groups = lax.axis_size("grp")
    token_count = tokens.shape[0]
    model_width = tokens.shape[1]
    slot_count = token_count // (2 * groups)
    spacing = EXPERTS // groups
    struck = routes % spacing == 0
    owners = jnp.sum(jnp.where(struck, routes // spacing, 0), axis=1)
    landed = jnp.any(struck, axis=1)
    weighting = jnp.sum(jnp.where(struck, route_gates, jnp.zeros_like(route_gates)), axis=1)
    chosen = ((owners[:, None] == jnp.arange(groups)[None, :]) & landed[:, None]).astype(jnp.int32)
    before = jnp.cumsum(chosen, axis=0) - chosen
    ranking = jnp.sum(before * chosen, axis=1)
    target = owners * slot_count + ranking
    placing = (
        (jnp.arange(groups * slot_count)[:, None] == target[None, :]) & landed[None, :]
    ).astype(jnp.bfloat16)
    outgoing = jnp.dot(placing, tokens, preferred_element_type=jnp.float32).astype(jnp.bfloat16)
    outgoing = outgoing.reshape(groups, slot_count, model_width)
    if groups == 4 and lax.axis_size("ing") == 2 and lax.axis_size("dp") == 2 and slot_count == 32:
        returned = expert_call(outgoing, gate_proj, up_proj, down_proj)
    else:
        returned = plain_call(outgoing, gate_proj, up_proj, down_proj)
    routed = jnp.einsum(
        "st,sd->td", placing, returned.reshape(-1, model_width), preferred_element_type=jnp.float32
    )
    return (weighting[:, None] * routed).astype(jnp.bfloat16)


def solution(mesh):
    placed = (
        P(("rep", "grp", "ing", "dp"), None),
        P(("rep", "grp", "ing", "dp"), None),
        P(("rep", "grp", "ing", "dp"), None),
        P("grp", None, ("ing", "dp")),
        P("grp", None, ("ing", "dp")),
        P("grp", ("ing", "dp"), None),
    )
    return jax.shard_map(
        on_device,
        mesh=mesh,
        in_specs=placed,
        out_specs=P(("rep", "grp", "ing", "dp"), None),
        check_vma=False,
    )
```

```python
import functools

import jax
import jax.numpy as jnp
from jax import lax
from jax.experimental import pallas as pl
from jax.experimental.pallas import tpu as pltpu
from jax.sharding import PartitionSpec as P

EXPERTS = 256
MESH = pl.DeviceIdType.MESH


def expert_rows(routed_rows, weight_set):
    gate_weight, up_weight, down_weight = weight_set
    gathered = lax.all_gather(routed_rows, "ing", axis=0, tiled=True)
    gate_act = jnp.dot(gathered, gate_weight[0], preferred_element_type=jnp.float32)
    up_act = jnp.dot(gathered, up_weight[0], preferred_element_type=jnp.float32)
    hidden = (jax.nn.silu(gate_act) * up_act).astype(jnp.bfloat16)
    return lax.psum_scatter(
        jnp.dot(hidden, down_weight[0], preferred_element_type=jnp.float32).astype(jnp.bfloat16),
        "ing",
        scatter_dimension=0,
        tiled=True,
    )


def swapped(z, d):
    flipped = z
    if d % 2:
        flipped = flipped + 1 - 2 * (z % 2)
    if d // 2:
        flipped = flipped + 2 - 4 * ((z // 2) % 2)
    return flipped


def expert_kernel(
    outgoing, gate_hbm, up_hbm, down_hbm, returned,
    gate_w, up_w, down_w, rows, kept, leaving, coming, summed,
    local_sem, weight_send, weight_recv, zin_send, zin_recv, xin_send, xin_recv,
    xout_send, xout_recv, zout_send, zout_recv,
):
    z, x, c = (lax.axis_index(name) for name in ("grp", "ing", "dp"))
    across, sibling = {"ing": 1 - x}, {"dp": 1 - c}
    half_rows, width = rows.shape[3], rows.shape[4]

    barrier = pltpu.get_barrier_semaphore()
    peers = [across, sibling] + [{"grp": swapped(z, d)} for d in (1, 2, 3)]
    for peer in peers:
        pl.semaphore_signal(barrier, inc=1, device_id=peer, device_id_type=MESH)
    pl.semaphore_wait(barrier, len(peers))

    def remote(src, dst, send, recv, to):
        return pltpu.make_async_remote_copy(
            src_ref=src, dst_ref=dst, send_sem=send, recv_sem=recv, device_id=to, device_id_type=MESH
        )

    def zin(d, h):
        t = swapped(z, d)
        return remote(outgoing.at[t, h], rows.at[d, h, 0], zin_send.at[d, h], zin_recv.at[d, h], {"grp": t})

    def xin(d, h):
        return remote(rows.at[d, h, 0], rows.at[d, h, 1], xin_send.at[d, h], xin_recv.at[d, h], across)

    def xout(d, h):
        return remote(leaving.at[d, h], coming.at[d, h], xout_send.at[d, h], xout_recv.at[d, h], across)

    def zout(d, h, t):
        return remote(summed.at[d, h], returned.at[z, h], zout_send.at[d, h], zout_recv.at[d, h], {"grp": t})

    def flipped(d):
        low, high = d % 2, d // 2
        return z + low * (1 - 2 * (z % 2)) + high * (2 - 4 * ((z // 2) % 2))

    for h in range(2):
        zin(2, h).start()
    for h in range(2):
        rows[0, h, 0] = outgoing[z, h]
        xin(0, h).start()
    for h in range(2):
        zin(1, h).start()
    weights = []
    for i, (hbm, vmem) in enumerate(((gate_hbm, gate_w), (up_hbm, up_w), (down_hbm, down_w))):
        own = pltpu.make_async_copy(hbm, vmem.at[0], local_sem.at[i])
        other = remote(hbm, vmem.at[1], weight_send.at[i], weight_recv.at[i], sibling)
        own.start()
        other.start()
        weights.append((own, other))
    for h in range(2):
        zin(2, h).wait_recv()
        xin(2, h).start()
        zin(3, h).start()
    for h in range(2):
        zin(1, h).wait_recv()
        xin(1, h).start()
    for own, other in weights[:2]:
        own.wait()
        other.wait_recv()

    def chunk_of(i):
        pair = i // 2
        return (1 - pair // 2) * (2 - pair) + (pair // 2) * 3 * (3 - pair), i % 2

    def finish(i):
        d, h = chunk_of(i)
        xout(d, h).wait_recv()
        summed[d, h] = (kept[d, h] + coming[d, h].astype(jnp.float32)).astype(jnp.bfloat16)

        @pl.when(d == 0)
        def _():
            pltpu.make_async_copy(summed.at[d, h], returned.at[z, h], local_sem.at[3 + h]).start()

        @pl.when(d != 0)
        def _():
            zout(d, h, flipped(d)).start()

    def compute(i, carry):
        d, h = chunk_of(i)
        xin(d, h).wait_recv()
        chunk = rows.at[d, h]
        tile = chunk[...].reshape(2 * half_rows, width)
        hidden = []
        for w in range(2):
            gate_act = jnp.dot(tile, gate_w[w], preferred_element_type=jnp.float32)
            up_act = jnp.dot(tile, up_w[w], preferred_element_type=jnp.float32)
            hidden.append((gate_act / (1.0 + jnp.exp(-gate_act)) * up_act).astype(jnp.bfloat16))

        @pl.when(i == 0)
        def _():
            weights[2][0].wait()
            weights[2][1].wait_recv()

        step = 1024

        def down(n, carry):
            columns = pl.ds(pl.multiple_of(n * step, step), step)
            part = jnp.dot(hidden[0], down_w[0, :, columns], preferred_element_type=jnp.float32)
            part += jnp.dot(hidden[1], down_w[1, :, columns], preferred_element_type=jnp.float32)
            kept[d, h, :, columns] = part[:half_rows]
            leaving[d, h, :, columns] = part[half_rows:].astype(jnp.bfloat16)
            return carry

        lax.fori_loop(0, width // step, down, 0)
        xout(d, h).start()

        @pl.when((i == 1) | (i == 3))
        def _():
            zin(3, i // 2).wait_recv()
            xin(3, i // 2).start()

        @pl.when(i >= 2)
        def _():
            finish(i - 2)

        return carry

    lax.fori_loop(0, 8, compute, 0)
    for i in (6, 7):
        finish(i)
    for own, other in weights:
        other.wait_send()
    for h in range(2):
        pltpu.make_async_copy(summed.at[0, h], returned.at[z, h], local_sem.at[3 + h]).wait()
        for d in range(4):
            xin(d, h).wait_send()
            xout(d, h).wait_send()
            if d:
                zin(d, h).wait_send()
                zout(d, h, swapped(z, d)).wait()


def expert_call(outgoing, gate_proj, up_proj, down_proj):
    groups, slot_count, model_width = outgoing.shape
    hidden = gate_proj.shape[2]
    halves = (groups, 2, slot_count // 2, model_width)
    dma = pltpu.SemaphoreType.DMA
    vmem, hbm = pl.BlockSpec(memory_space=pltpu.VMEM), pl.BlockSpec(memory_space=pl.ANY)
    bf16, f32 = jnp.bfloat16, jnp.float32
    returned = pl.pallas_call(
        expert_kernel,
        out_shape=jax.ShapeDtypeStruct(halves, bf16),
        in_specs=[vmem, hbm, hbm, hbm],
        out_specs=hbm,
        scratch_shapes=[
            pltpu.VMEM((2, model_width, hidden), bf16),
            pltpu.VMEM((2, model_width, hidden), bf16),
            pltpu.VMEM((2, hidden, model_width), bf16),
            pltpu.VMEM((groups, 2, 2, slot_count // 2, model_width), bf16),
            pltpu.VMEM(halves, f32),
            pltpu.VMEM(halves, bf16),
            pltpu.VMEM(halves, bf16),
            pltpu.VMEM(halves, bf16),
            dma((5,)),
            dma((3,)),
            dma((3,)),
        ]
        + [dma((groups, 2))] * 8,
        compiler_params=pltpu.CompilerParams(
            collective_id=0, has_side_effects=True, vmem_limit_bytes=56 * 2**20
        ),
        name="routed_experts",
    )(outgoing.reshape(halves), gate_proj[0], up_proj[0], down_proj[0])
    return returned.reshape(groups, slot_count, model_width)


def plain_call(outgoing, gate_proj, up_proj, down_proj):
    groups, slot_count, model_width = outgoing.shape
    arrived = lax.all_to_all(outgoing, "grp", split_axis=0, concat_axis=0, tiled=True)
    weight_set = (
        lax.all_gather(gate_proj, "dp", axis=2, tiled=True),
        lax.all_gather(up_proj, "dp", axis=2, tiled=True),
        lax.all_gather(down_proj, "dp", axis=1, tiled=True),
    )
    results = expert_rows(arrived.reshape(-1, model_width), weight_set).reshape(
        groups, slot_count, model_width
    )
    return lax.all_to_all(results, "grp", split_axis=0, concat_axis=0, tiled=True)


def on_device(tokens, routes, route_gates, gate_proj, up_proj, down_proj):
    groups = lax.axis_size("grp")
    token_count = tokens.shape[0]
    model_width = tokens.shape[1]
    slot_count = token_count // (2 * groups)
    spacing = EXPERTS // groups
    struck = routes % spacing == 0
    owners = jnp.sum(jnp.where(struck, routes // spacing, 0), axis=1)
    landed = jnp.any(struck, axis=1)
    weighting = jnp.sum(jnp.where(struck, route_gates, jnp.zeros_like(route_gates)), axis=1)
    order = jnp.arange(token_count)
    earlier = (owners[:, None] == owners[None, :]) & landed[:, None] & (order[:, None] < order[None, :])
    ranking = jnp.sum(earlier.astype(jnp.int32), axis=0)
    target = owners * slot_count + ranking
    placing = (
        (jnp.arange(groups * slot_count)[:, None] == target[None, :]) & landed[None, :]
    ).astype(jnp.bfloat16)
    outgoing = jnp.dot(placing, tokens, preferred_element_type=jnp.float32).astype(jnp.bfloat16)
    outgoing = outgoing.reshape(groups, slot_count, model_width)
    if groups == 4 and lax.axis_size("ing") == 2 and lax.axis_size("dp") == 2 and slot_count == 32:
        returned = expert_call(outgoing, gate_proj, up_proj, down_proj)
    else:
        returned = plain_call(outgoing, gate_proj, up_proj, down_proj)
    placed_back = (
        (target[:, None] == jnp.arange(groups * slot_count)[None, :]) & landed[:, None]
    ).astype(jnp.bfloat16)
    routed = jnp.einsum(
        "ts,sd->td", placed_back, returned.reshape(-1, model_width), preferred_element_type=jnp.float32
    )
    return (weighting[:, None] * routed).astype(jnp.bfloat16)


def solution(mesh):
    placed = (
        P(("rep", "grp", "ing", "dp"), None),
        P(("rep", "grp", "ing", "dp"), None),
        P(("rep", "grp", "ing", "dp"), None),
        P("grp", None, ("ing", "dp")),
        P("grp", None, ("ing", "dp")),
        P("grp", ("ing", "dp"), None),
    )
    return jax.shard_map(
        on_device,
        mesh=mesh,
        in_specs=placed,
        out_specs=P(("rep", "grp", "ing", "dp"), None),
        check_vma=False,
    )
```

```python
import functools

import jax
import jax.numpy as jnp
from jax import lax
from jax.experimental import pallas as pl
from jax.experimental.pallas import tpu as pltpu
from jax.sharding import PartitionSpec as P

EXPERTS = 256
MESH = pl.DeviceIdType.MESH


def expert_rows(routed_rows, weight_set):
    gate_weight, up_weight, down_weight = weight_set
    gathered = lax.all_gather(routed_rows, "ing", axis=0, tiled=True)
    gate_act = jnp.dot(gathered, gate_weight[0], preferred_element_type=jnp.float32)
    up_act = jnp.dot(gathered, up_weight[0], preferred_element_type=jnp.float32)
    hidden = (jax.nn.silu(gate_act) * up_act).astype(jnp.bfloat16)
    return lax.psum_scatter(
        jnp.dot(hidden, down_weight[0], preferred_element_type=jnp.float32).astype(jnp.bfloat16),
        "ing",
        scatter_dimension=0,
        tiled=True,
    )


def swapped(z, d):
    flipped = z
    if d % 2:
        flipped = flipped + 1 - 2 * (z % 2)
    if d // 2:
        flipped = flipped + 2 - 4 * ((z // 2) % 2)
    return flipped


def expert_kernel(
    tokens, placing, gate_hbm, up_hbm, down_hbm, returned,
    outgoing, gate_w, up_w, down_w, rows, kept, leaving, coming, summed,
    local_sem, weight_send, weight_recv, zin_send, zin_recv, xin_send, xin_recv,
    xout_send, xout_recv, zout_send, zout_recv,
):
    z, x, c = (lax.axis_index(name) for name in ("grp", "ing", "dp"))
    across, sibling = {"ing": 1 - x}, {"dp": 1 - c}
    half_rows, width = rows.shape[3], rows.shape[4]

    barrier = pltpu.get_barrier_semaphore()
    peers = [across, sibling] + [{"grp": swapped(z, d)} for d in (1, 2, 3)]
    for peer in peers:
        pl.semaphore_signal(barrier, inc=1, device_id=peer, device_id_type=MESH)
    pl.semaphore_wait(barrier, len(peers))

    def remote(src, dst, send, recv, to):
        return pltpu.make_async_remote_copy(
            src_ref=src, dst_ref=dst, send_sem=send, recv_sem=recv, device_id=to, device_id_type=MESH
        )

    def zin(d, h):
        t = swapped(z, d)
        return remote(outgoing.at[t, h], rows.at[d, h, 0], zin_send.at[d, h], zin_recv.at[d, h], {"grp": t})

    def xin(d, h):
        return remote(rows.at[d, h, 0], rows.at[d, h, 1], xin_send.at[d, h], xin_recv.at[d, h], across)

    def xout(d, h):
        return remote(leaving.at[d, h], coming.at[d, h], xout_send.at[d, h], xout_recv.at[d, h], across)

    def zout(d, h, t):
        return remote(summed.at[d, h], returned.at[z, h], zout_send.at[d, h], zout_recv.at[d, h], {"grp": t})

    def flipped(d):
        low, high = d % 2, d // 2
        return z + low * (1 - 2 * (z % 2)) + high * (2 - 4 * ((z // 2) % 2))

    step = 1024

    def gather(t, place):
        picked = placing[t].reshape(2 * half_rows, placing.shape[3])

        def one(n, carry):
            columns = pl.ds(pl.multiple_of(n * step, step), step)
            found = jnp.dot(picked, tokens[:, columns], preferred_element_type=jnp.float32)
            found = found.astype(jnp.bfloat16)
            for h in range(2):
                place(h)[:, columns] = found[h * half_rows : (h + 1) * half_rows]
            return carry

        lax.fori_loop(0, width // step, one, 0)

    gather(z, lambda h: rows.at[0, h, 0])
    for h in range(2):
        xin(0, h).start()
    for d in (2, 1):
        t = swapped(z, d)
        gather(t, lambda h: outgoing.at[t, h])
        for h in range(2):
            zin(d, h).start()
    weights = []
    for i, (hbm, vmem) in enumerate(((gate_hbm, gate_w), (up_hbm, up_w), (down_hbm, down_w))):
        own = pltpu.make_async_copy(hbm, vmem.at[0], local_sem.at[i])
        other = remote(hbm, vmem.at[1], weight_send.at[i], weight_recv.at[i], sibling)
        own.start()
        other.start()
        weights.append((own, other))
    far = swapped(z, 3)
    gather(far, lambda h: outgoing.at[far, h])
    for h in range(2):
        zin(2, h).wait_recv()
        xin(2, h).start()
        zin(3, h).start()
    for h in range(2):
        zin(1, h).wait_recv()
        xin(1, h).start()
    for own, other in weights[:2]:
        own.wait()
        other.wait_recv()

    def chunk_of(i):
        pair = i // 2
        return (1 - pair // 2) * (2 - pair) + (pair // 2) * 3 * (3 - pair), i % 2

    def finish(i):
        d, h = chunk_of(i)
        xout(d, h).wait_recv()
        summed[d, h] = (kept[d, h] + coming[d, h].astype(jnp.float32)).astype(jnp.bfloat16)

        @pl.when(d == 0)
        def _():
            pltpu.make_async_copy(summed.at[d, h], returned.at[z, h], local_sem.at[3 + h]).start()

        @pl.when(d != 0)
        def _():
            zout(d, h, flipped(d)).start()

    def compute(i, carry):
        d, h = chunk_of(i)
        xin(d, h).wait_recv()
        chunk = rows.at[d, h]
        tile = chunk[...].reshape(2 * half_rows, width)
        hidden = []
        for w in range(2):
            gate_act = jnp.dot(tile, gate_w[w], preferred_element_type=jnp.float32)
            up_act = jnp.dot(tile, up_w[w], preferred_element_type=jnp.float32)
            hidden.append((gate_act / (1.0 + jnp.exp(-gate_act)) * up_act).astype(jnp.bfloat16))

        @pl.when(i == 0)
        def _():
            weights[2][0].wait()
            weights[2][1].wait_recv()

        def down(n, carry):
            columns = pl.ds(pl.multiple_of(n * step, step), step)
            part = jnp.dot(hidden[0], down_w[0, :, columns], preferred_element_type=jnp.float32)
            part += jnp.dot(hidden[1], down_w[1, :, columns], preferred_element_type=jnp.float32)
            kept[d, h, :, columns] = part[:half_rows]
            leaving[d, h, :, columns] = part[half_rows:].astype(jnp.bfloat16)
            return carry

        lax.fori_loop(0, width // step, down, 0)
        xout(d, h).start()

        @pl.when((i == 1) | (i == 3))
        def _():
            zin(3, i // 2).wait_recv()
            xin(3, i // 2).start()

        @pl.when(i >= 2)
        def _():
            finish(i - 2)

        return carry

    lax.fori_loop(0, 8, compute, 0)
    for i in (6, 7):
        finish(i)
    for own, other in weights:
        other.wait_send()
    for h in range(2):
        pltpu.make_async_copy(summed.at[0, h], returned.at[z, h], local_sem.at[3 + h]).wait()
        for d in range(4):
            xin(d, h).wait_send()
            xout(d, h).wait_send()
            if d:
                zin(d, h).wait_send()
                zout(d, h, swapped(z, d)).wait()


def expert_call(tokens, placing, groups, gate_proj, up_proj, down_proj):
    token_count, model_width = tokens.shape
    slot_count = placing.shape[0] // groups
    hidden = gate_proj.shape[2]
    halves = (groups, 2, slot_count // 2, model_width)
    dma = pltpu.SemaphoreType.DMA
    vmem, hbm = pl.BlockSpec(memory_space=pltpu.VMEM), pl.BlockSpec(memory_space=pl.ANY)
    bf16, f32 = jnp.bfloat16, jnp.float32
    returned = pl.pallas_call(
        expert_kernel,
        out_shape=jax.ShapeDtypeStruct(halves, bf16),
        in_specs=[vmem, vmem, hbm, hbm, hbm],
        out_specs=hbm,
        scratch_shapes=[
            pltpu.VMEM(halves, bf16),
            pltpu.VMEM((2, model_width, hidden), bf16),
            pltpu.VMEM((2, model_width, hidden), bf16),
            pltpu.VMEM((2, hidden, model_width), bf16),
            pltpu.VMEM((groups, 2, 2, slot_count // 2, model_width), bf16),
            pltpu.VMEM(halves, f32),
            pltpu.VMEM(halves, bf16),
            pltpu.VMEM(halves, bf16),
            pltpu.VMEM(halves, bf16),
            dma((5,)),
            dma((3,)),
            dma((3,)),
        ]
        + [dma((groups, 2))] * 8,
        compiler_params=pltpu.CompilerParams(
            collective_id=0, has_side_effects=True, vmem_limit_bytes=56 * 2**20
        ),
        name="routed_experts",
    )(tokens, placing.reshape(halves[:3] + (token_count,)), gate_proj[0], up_proj[0], down_proj[0])
    return returned.reshape(groups, slot_count, model_width)


def plain_call(tokens, placing, groups, gate_proj, up_proj, down_proj):
    model_width = tokens.shape[1]
    slot_count = placing.shape[0] // groups
    outgoing = jnp.dot(placing, tokens, preferred_element_type=jnp.float32).astype(jnp.bfloat16)
    outgoing = outgoing.reshape(groups, slot_count, model_width)
    arrived = lax.all_to_all(outgoing, "grp", split_axis=0, concat_axis=0, tiled=True)
    weight_set = (
        lax.all_gather(gate_proj, "dp", axis=2, tiled=True),
        lax.all_gather(up_proj, "dp", axis=2, tiled=True),
        lax.all_gather(down_proj, "dp", axis=1, tiled=True),
    )
    results = expert_rows(arrived.reshape(-1, model_width), weight_set).reshape(
        groups, slot_count, model_width
    )
    return lax.all_to_all(results, "grp", split_axis=0, concat_axis=0, tiled=True)


def on_device(tokens, routes, route_gates, gate_proj, up_proj, down_proj):
    groups = lax.axis_size("grp")
    token_count = tokens.shape[0]
    model_width = tokens.shape[1]
    slot_count = token_count // (2 * groups)
    spacing = EXPERTS // groups
    struck = routes % spacing == 0
    owners = jnp.sum(jnp.where(struck, routes // spacing, 0), axis=1)
    landed = jnp.any(struck, axis=1)
    weighting = jnp.sum(jnp.where(struck, route_gates, jnp.zeros_like(route_gates)), axis=1)
    order = jnp.arange(token_count)
    earlier = (owners[:, None] == owners[None, :]) & landed[:, None] & (order[:, None] < order[None, :])
    ranking = jnp.sum(earlier.astype(jnp.int32), axis=0)
    target = owners * slot_count + ranking
    placing = (
        (jnp.arange(groups * slot_count)[:, None] == target[None, :]) & landed[None, :]
    ).astype(jnp.bfloat16)
    if groups == 4 and lax.axis_size("ing") == 2 and lax.axis_size("dp") == 2 and slot_count == 32:
        returned = expert_call(tokens, placing, groups, gate_proj, up_proj, down_proj)
    else:
        returned = plain_call(tokens, placing, groups, gate_proj, up_proj, down_proj)
    placed_back = (
        (target[:, None] == jnp.arange(groups * slot_count)[None, :]) & landed[:, None]
    ).astype(jnp.bfloat16)
    routed = jnp.einsum(
        "ts,sd->td", placed_back, returned.reshape(-1, model_width), preferred_element_type=jnp.float32
    )
    return (weighting[:, None] * routed).astype(jnp.bfloat16)


def solution(mesh):
    placed = (
        P(("rep", "grp", "ing", "dp"), None),
        P(("rep", "grp", "ing", "dp"), None),
        P(("rep", "grp", "ing", "dp"), None),
        P("grp", None, ("ing", "dp")),
        P("grp", None, ("ing", "dp")),
        P("grp", ("ing", "dp"), None),
    )
    return jax.shard_map(
        on_device,
        mesh=mesh,
        in_specs=placed,
        out_specs=P(("rep", "grp", "ing", "dp"), None),
        check_vma=False,
    )
```

```python
import functools

import jax
import jax.numpy as jnp
from jax import lax
from jax.experimental import pallas as pl
from jax.experimental.pallas import tpu as pltpu
from jax.sharding import PartitionSpec as P

EXPERTS = 256
MESH = pl.DeviceIdType.MESH


def expert_rows(routed_rows, weight_set):
    gate_weight, up_weight, down_weight = weight_set
    gathered = lax.all_gather(routed_rows, "ing", axis=0, tiled=True)
    gate_act = jnp.dot(gathered, gate_weight[0], preferred_element_type=jnp.float32)
    up_act = jnp.dot(gathered, up_weight[0], preferred_element_type=jnp.float32)
    hidden = (jax.nn.silu(gate_act) * up_act).astype(jnp.bfloat16)
    return lax.psum_scatter(
        jnp.dot(hidden, down_weight[0], preferred_element_type=jnp.float32).astype(jnp.bfloat16),
        "ing",
        scatter_dimension=0,
        tiled=True,
    )


def swapped(z, d):
    flipped = z
    if d % 2:
        flipped = flipped + 1 - 2 * (z % 2)
    if d // 2:
        flipped = flipped + 2 - 4 * ((z // 2) % 2)
    return flipped


def expert_kernel(
    outgoing, gate_hbm, up_hbm, down_hbm, returned,
    gate_w, up_w, down_w, rows, kept, leaving, coming, summed,
    local_sem, weight_send, weight_recv, zin_send, zin_recv, xin_send, xin_recv,
    xout_send, xout_recv, zout_send, zout_recv,
):
    z, x, c = (lax.axis_index(name) for name in ("grp", "ing", "dp"))
    across, sibling = {"ing": 1 - x}, {"dp": 1 - c}
    half_rows, width = rows.shape[3], rows.shape[4]

    barrier = pltpu.get_barrier_semaphore()
    peers = [across, sibling] + [{"grp": swapped(z, d)} for d in (1, 2, 3)]
    for peer in peers:
        pl.semaphore_signal(barrier, inc=1, device_id=peer, device_id_type=MESH)
    pl.semaphore_wait(barrier, len(peers))

    def remote(src, dst, send, recv, to):
        return pltpu.make_async_remote_copy(
            src_ref=src, dst_ref=dst, send_sem=send, recv_sem=recv, device_id=to, device_id_type=MESH
        )

    def zin(d, h):
        t = swapped(z, d)
        return remote(outgoing.at[t, h], rows.at[d, h, 0], zin_send.at[d, h], zin_recv.at[d, h], {"grp": t})

    def xin(d, h):
        return remote(rows.at[d, h, 0], rows.at[d, h, 1], xin_send.at[d, h], xin_recv.at[d, h], across)

    def xout(d, h):
        return remote(leaving.at[d, h], coming.at[d, h], xout_send.at[d, h], xout_recv.at[d, h], across)

    def zout(d, h, t):
        return remote(summed.at[d, h], returned.at[z, h], zout_send.at[d, h], zout_recv.at[d, h], {"grp": t})

    def flipped(d):
        low, high = d % 2, d // 2
        return z + low * (1 - 2 * (z % 2)) + high * (2 - 4 * ((z // 2) % 2))

    for h in range(2):
        zin(2, h).start()
    for h in range(2):
        rows[0, h, 0] = outgoing[z, h]
        xin(0, h).start()
    for h in range(2):
        zin(1, h).start()
    weights = []
    for i, (hbm, vmem) in enumerate(((gate_hbm, gate_w), (up_hbm, up_w), (down_hbm, down_w))):
        own = pltpu.make_async_copy(hbm, vmem.at[0], local_sem.at[i])
        other = remote(hbm, vmem.at[1], weight_send.at[i], weight_recv.at[i], sibling)
        own.start()
        other.start()
        weights.append((own, other))
    for h in range(2):
        zin(2, h).wait_recv()
        xin(2, h).start()
        zin(3, h).start()
    for h in range(2):
        zin(1, h).wait_recv()
        xin(1, h).start()
    for own, other in weights[:2]:
        own.wait()
        other.wait_recv()

    def distance(p):
        return (1 - p // 2) * (2 - p) + (p // 2) * 3 * (3 - p)

    def finish(p):
        d = distance(p)
        for h in range(2):
            xout(d, h).wait_recv()
            summed[d, h] = (kept[d, h] + coming[d, h].astype(jnp.float32)).astype(jnp.bfloat16)

            @pl.when(d == 0)
            def _():
                pltpu.make_async_copy(summed.at[d, h], returned.at[z, h], local_sem.at[3 + h]).start()

            @pl.when(d != 0)
            def _():
                zout(d, h, flipped(d)).start()

    def compute(p, carry):
        d = distance(p)
        for h in range(2):
            xin(d, h).wait_recv()
        tile = rows[d].reshape(4 * half_rows, width)
        hidden = []
        for w in range(2):
            gate_act = jnp.dot(tile, gate_w[w], preferred_element_type=jnp.float32)
            up_act = jnp.dot(tile, up_w[w], preferred_element_type=jnp.float32)
            hidden.append((gate_act / (1.0 + jnp.exp(-gate_act)) * up_act).astype(jnp.bfloat16))

        @pl.when(p == 0)
        def _():
            weights[2][0].wait()
            weights[2][1].wait_recv()

        step = 1024

        def down(n, carry):
            columns = pl.ds(pl.multiple_of(n * step, step), step)
            part = jnp.dot(hidden[0], down_w[0, :, columns], preferred_element_type=jnp.float32)
            part += jnp.dot(hidden[1], down_w[1, :, columns], preferred_element_type=jnp.float32)
            for h in range(2):
                mine, theirs = 2 * h * half_rows, (2 * h + 1) * half_rows
                kept[d, h, :, columns] = part[mine : mine + half_rows]
                leaving[d, h, :, columns] = part[theirs : theirs + half_rows].astype(jnp.bfloat16)
            return carry

        lax.fori_loop(0, width // step, down, 0)
        for h in range(2):
            xout(d, h).start()

        @pl.when(p < 2)
        def _():
            zin(3, p).wait_recv()
            xin(3, p).start()

        @pl.when(p >= 1)
        def _():
            finish(p - 1)

        return carry

    lax.fori_loop(0, 4, compute, 0)
    finish(3)
    for own, other in weights:
        other.wait_send()
    for h in range(2):
        pltpu.make_async_copy(summed.at[0, h], returned.at[z, h], local_sem.at[3 + h]).wait()
        for d in range(4):
            xin(d, h).wait_send()
            xout(d, h).wait_send()
            if d:
                zin(d, h).wait_send()
                zout(d, h, swapped(z, d)).wait()


def expert_call(outgoing, gate_proj, up_proj, down_proj):
    groups, slot_count, model_width = outgoing.shape
    hidden = gate_proj.shape[2]
    halves = (groups, 2, slot_count // 2, model_width)
    dma = pltpu.SemaphoreType.DMA
    vmem, hbm = pl.BlockSpec(memory_space=pltpu.VMEM), pl.BlockSpec(memory_space=pl.ANY)
    bf16, f32 = jnp.bfloat16, jnp.float32
    returned = pl.pallas_call(
        expert_kernel,
        out_shape=jax.ShapeDtypeStruct(halves, bf16),
        in_specs=[vmem, hbm, hbm, hbm],
        out_specs=hbm,
        scratch_shapes=[
            pltpu.VMEM((2, model_width, hidden), bf16),
            pltpu.VMEM((2, model_width, hidden), bf16),
            pltpu.VMEM((2, hidden, model_width), bf16),
            pltpu.VMEM((groups, 2, 2, slot_count // 2, model_width), bf16),
            pltpu.VMEM(halves, f32),
            pltpu.VMEM(halves, bf16),
            pltpu.VMEM(halves, bf16),
            pltpu.VMEM(halves, bf16),
            dma((5,)),
            dma((3,)),
            dma((3,)),
        ]
        + [dma((groups, 2))] * 8,
        compiler_params=pltpu.CompilerParams(
            collective_id=0, has_side_effects=True, vmem_limit_bytes=56 * 2**20
        ),
        name="routed_experts",
    )(outgoing.reshape(halves), gate_proj[0], up_proj[0], down_proj[0])
    return returned.reshape(groups, slot_count, model_width)


def plain_call(outgoing, gate_proj, up_proj, down_proj):
    groups, slot_count, model_width = outgoing.shape
    arrived = lax.all_to_all(outgoing, "grp", split_axis=0, concat_axis=0, tiled=True)
    weight_set = (
        lax.all_gather(gate_proj, "dp", axis=2, tiled=True),
        lax.all_gather(up_proj, "dp", axis=2, tiled=True),
        lax.all_gather(down_proj, "dp", axis=1, tiled=True),
    )
    results = expert_rows(arrived.reshape(-1, model_width), weight_set).reshape(
        groups, slot_count, model_width
    )
    return lax.all_to_all(results, "grp", split_axis=0, concat_axis=0, tiled=True)


def on_device(tokens, routes, route_gates, gate_proj, up_proj, down_proj):
    groups = lax.axis_size("grp")
    token_count = tokens.shape[0]
    model_width = tokens.shape[1]
    slot_count = token_count // (2 * groups)
    spacing = EXPERTS // groups
    struck = routes % spacing == 0
    owners = jnp.sum(jnp.where(struck, routes // spacing, 0), axis=1)
    landed = jnp.any(struck, axis=1)
    weighting = jnp.sum(jnp.where(struck, route_gates, jnp.zeros_like(route_gates)), axis=1)
    order = jnp.arange(token_count)
    earlier = (owners[:, None] == owners[None, :]) & landed[:, None] & (order[:, None] < order[None, :])
    ranking = jnp.sum(earlier.astype(jnp.int32), axis=0)
    target = owners * slot_count + ranking
    placing = (
        (jnp.arange(groups * slot_count)[:, None] == target[None, :]) & landed[None, :]
    ).astype(jnp.bfloat16)
    outgoing = jnp.dot(placing, tokens, preferred_element_type=jnp.float32).astype(jnp.bfloat16)
    outgoing = outgoing.reshape(groups, slot_count, model_width)
    if groups == 4 and lax.axis_size("ing") == 2 and lax.axis_size("dp") == 2 and slot_count == 32:
        returned = expert_call(outgoing, gate_proj, up_proj, down_proj)
    else:
        returned = plain_call(outgoing, gate_proj, up_proj, down_proj)
    placed_back = (
        (target[:, None] == jnp.arange(groups * slot_count)[None, :]) & landed[:, None]
    ).astype(jnp.bfloat16)
    routed = jnp.einsum(
        "ts,sd->td", placed_back, returned.reshape(-1, model_width), preferred_element_type=jnp.float32
    )
    return (weighting[:, None] * routed).astype(jnp.bfloat16)


def solution(mesh):
    placed = (
        P(("rep", "grp", "ing", "dp"), None),
        P(("rep", "grp", "ing", "dp"), None),
        P(("rep", "grp", "ing", "dp"), None),
        P("grp", None, ("ing", "dp")),
        P("grp", None, ("ing", "dp")),
        P("grp", ("ing", "dp"), None),
    )
    return jax.shard_map(
        on_device,
        mesh=mesh,
        in_specs=placed,
        out_specs=P(("rep", "grp", "ing", "dp"), None),
        check_vma=False,
    )
```

```python
import functools

import jax
import jax.numpy as jnp
from jax import lax
from jax.experimental import pallas as pl
from jax.experimental.pallas import tpu as pltpu
from jax.sharding import PartitionSpec as P

EXPERTS = 256
MESH = pl.DeviceIdType.MESH


def expert_rows(routed_rows, weight_set):
    gate_weight, up_weight, down_weight = weight_set
    gathered = lax.all_gather(routed_rows, "ing", axis=0, tiled=True)
    gate_act = jnp.dot(gathered, gate_weight[0], preferred_element_type=jnp.float32)
    up_act = jnp.dot(gathered, up_weight[0], preferred_element_type=jnp.float32)
    hidden = (jax.nn.silu(gate_act) * up_act).astype(jnp.bfloat16)
    return lax.psum_scatter(
        jnp.dot(hidden, down_weight[0], preferred_element_type=jnp.float32).astype(jnp.bfloat16),
        "ing",
        scatter_dimension=0,
        tiled=True,
    )


def swapped(z, d):
    flipped = z
    if d % 2:
        flipped = flipped + 1 - 2 * (z % 2)
    if d // 2:
        flipped = flipped + 2 - 4 * ((z // 2) % 2)
    return flipped


def expert_kernel(
    outgoing, gate_hbm, up_hbm, down_hbm, returned,
    gate_w, up_w, down_w, rows, kept, leaving, coming, summed,
    local_sem, weight_send, weight_recv, zin_send, zin_recv, xin_send, xin_recv,
    xout_send, xout_recv, zout_send, zout_recv,
):
    z, x, c = (lax.axis_index(name) for name in ("grp", "ing", "dp"))
    across, sibling = {"ing": 1 - x}, {"dp": 1 - c}
    half_rows, width = rows.shape[3], rows.shape[4]

    barrier = pltpu.get_barrier_semaphore()
    peers = [across, sibling] + [{"grp": swapped(z, d)} for d in (1, 2, 3)]
    for peer in peers:
        pl.semaphore_signal(barrier, inc=1, device_id=peer, device_id_type=MESH)
    pl.semaphore_wait(barrier, len(peers))

    def remote(src, dst, send, recv, to):
        return pltpu.make_async_remote_copy(
            src_ref=src, dst_ref=dst, send_sem=send, recv_sem=recv, device_id=to, device_id_type=MESH
        )

    def zin(d, h):
        t = swapped(z, d)
        return remote(outgoing.at[t, h], rows.at[d, h, 0], zin_send.at[d, h], zin_recv.at[d, h], {"grp": t})

    def xin(d, h):
        return remote(rows.at[d, h, 0], rows.at[d, h, 1], xin_send.at[d, h], xin_recv.at[d, h], across)

    def xout(d, h):
        return remote(leaving.at[d, h], coming.at[d, h], xout_send.at[d, h], xout_recv.at[d, h], across)

    def zout(d, h, t):
        return remote(summed.at[d, h], returned.at[z, h], zout_send.at[d, h], zout_recv.at[d, h], {"grp": t})

    def flipped(d):
        low, high = d % 2, d // 2
        return z + low * (1 - 2 * (z % 2)) + high * (2 - 4 * ((z // 2) % 2))

    weights = []
    for i, (hbm, vmem) in enumerate(((gate_hbm, gate_w), (up_hbm, up_w), (down_hbm, down_w))):
        own = pltpu.make_async_copy(hbm, vmem.at[0], local_sem.at[i])
        other = remote(hbm, vmem.at[1], weight_send.at[i], weight_recv.at[i], sibling)
        own.start()
        other.start()
        weights.append((own, other))
    for h in range(2):
        zin(1, h).start()
    for h in range(2):
        zin(2, h).start()
    for h in range(2):
        rows[0, h, 0] = outgoing[z, h]
        xin(0, h).start()
    for h in range(2):
        zin(1, h).wait_recv()
        xin(1, h).start()
    for h in range(2):
        zin(2, h).wait_recv()
        xin(2, h).start()
        zin(3, h).start()
    for own, other in weights[:2]:
        own.wait()
        other.wait_recv()

    def chunk_of(i):
        pair = i // 2
        return (pair + 1) % 4, i % 2

    def finish(i):
        d, h = chunk_of(i)
        xout(d, h).wait_recv()
        summed[d, h] = (kept[d, h] + coming[d, h].astype(jnp.float32)).astype(jnp.bfloat16)

        @pl.when(d == 0)
        def _():
            pltpu.make_async_copy(summed.at[d, h], returned.at[z, h], local_sem.at[3 + h]).start()

        @pl.when(d != 0)
        def _():
            zout(d, h, flipped(d)).start()

    def compute(i, carry):
        d, h = chunk_of(i)
        xin(d, h).wait_recv()
        chunk = rows.at[d, h]
        tile = chunk[...].reshape(2 * half_rows, width)
        hidden = []
        for w in range(2):
            gate_act = jnp.dot(tile, gate_w[w], preferred_element_type=jnp.float32)
            up_act = jnp.dot(tile, up_w[w], preferred_element_type=jnp.float32)
            hidden.append((gate_act / (1.0 + jnp.exp(-gate_act)) * up_act).astype(jnp.bfloat16))

        @pl.when(i == 0)
        def _():
            weights[2][0].wait()
            weights[2][1].wait_recv()

        step = 1024

        def down(n, carry):
            columns = pl.ds(pl.multiple_of(n * step, step), step)
            part = jnp.dot(hidden[0], down_w[0, :, columns], preferred_element_type=jnp.float32)
            part += jnp.dot(hidden[1], down_w[1, :, columns], preferred_element_type=jnp.float32)
            kept[d, h, :, columns] = part[:half_rows]
            leaving[d, h, :, columns] = part[half_rows:].astype(jnp.bfloat16)
            return carry

        lax.fori_loop(0, width // step, down, 0)
        xout(d, h).start()

        @pl.when((i == 1) | (i == 3))
        def _():
            zin(3, i // 2).wait_recv()
            xin(3, i // 2).start()

        @pl.when(i >= 2)
        def _():
            finish(i - 2)

        return carry

    lax.fori_loop(0, 8, compute, 0)
    for i in (6, 7):
        finish(i)
    for own, other in weights:
        other.wait_send()
    for h in range(2):
        pltpu.make_async_copy(summed.at[0, h], returned.at[z, h], local_sem.at[3 + h]).wait()
        for d in range(4):
            xin(d, h).wait_send()
            xout(d, h).wait_send()
            if d:
                zin(d, h).wait_send()
                zout(d, h, swapped(z, d)).wait()


def expert_call(outgoing, gate_proj, up_proj, down_proj):
    groups, slot_count, model_width = outgoing.shape
    hidden = gate_proj.shape[2]
    halves = (groups, 2, slot_count // 2, model_width)
    dma = pltpu.SemaphoreType.DMA
    vmem, hbm = pl.BlockSpec(memory_space=pltpu.VMEM), pl.BlockSpec(memory_space=pl.ANY)
    bf16, f32 = jnp.bfloat16, jnp.float32
    returned = pl.pallas_call(
        expert_kernel,
        out_shape=jax.ShapeDtypeStruct(halves, bf16),
        in_specs=[vmem, hbm, hbm, hbm],
        out_specs=hbm,
        scratch_shapes=[
            pltpu.VMEM((2, model_width, hidden), bf16),
            pltpu.VMEM((2, model_width, hidden), bf16),
            pltpu.VMEM((2, hidden, model_width), bf16),
            pltpu.VMEM((groups, 2, 2, slot_count // 2, model_width), bf16),
            pltpu.VMEM(halves, f32),
            pltpu.VMEM(halves, bf16),
            pltpu.VMEM(halves, bf16),
            pltpu.VMEM(halves, bf16),
            dma((5,)),
            dma((3,)),
            dma((3,)),
        ]
        + [dma((groups, 2))] * 8,
        compiler_params=pltpu.CompilerParams(
            collective_id=0, has_side_effects=True, vmem_limit_bytes=56 * 2**20
        ),
        name="routed_experts",
    )(outgoing.reshape(halves), gate_proj[0], up_proj[0], down_proj[0])
    return returned.reshape(groups, slot_count, model_width)


def plain_call(outgoing, gate_proj, up_proj, down_proj):
    groups, slot_count, model_width = outgoing.shape
    arrived = lax.all_to_all(outgoing, "grp", split_axis=0, concat_axis=0, tiled=True)
    weight_set = (
        lax.all_gather(gate_proj, "dp", axis=2, tiled=True),
        lax.all_gather(up_proj, "dp", axis=2, tiled=True),
        lax.all_gather(down_proj, "dp", axis=1, tiled=True),
    )
    results = expert_rows(arrived.reshape(-1, model_width), weight_set).reshape(
        groups, slot_count, model_width
    )
    return lax.all_to_all(results, "grp", split_axis=0, concat_axis=0, tiled=True)


def on_device(tokens, routes, route_gates, gate_proj, up_proj, down_proj):
    groups = lax.axis_size("grp")
    token_count = tokens.shape[0]
    model_width = tokens.shape[1]
    slot_count = token_count // (2 * groups)
    spacing = EXPERTS // groups
    struck = routes % spacing == 0
    owners = jnp.sum(jnp.where(struck, routes // spacing, 0), axis=1)
    landed = jnp.any(struck, axis=1)
    weighting = jnp.sum(jnp.where(struck, route_gates, jnp.zeros_like(route_gates)), axis=1)
    order = jnp.arange(token_count)
    earlier = (owners[:, None] == owners[None, :]) & landed[:, None] & (order[:, None] < order[None, :])
    ranking = jnp.sum(earlier.astype(jnp.int32), axis=0)
    target = owners * slot_count + ranking
    placing = (
        (jnp.arange(groups * slot_count)[:, None] == target[None, :]) & landed[None, :]
    ).astype(jnp.bfloat16)
    outgoing = jnp.dot(placing, tokens, preferred_element_type=jnp.float32).astype(jnp.bfloat16)
    outgoing = outgoing.reshape(groups, slot_count, model_width)
    if groups == 4 and lax.axis_size("ing") == 2 and lax.axis_size("dp") == 2 and slot_count == 32:
        returned = expert_call(outgoing, gate_proj, up_proj, down_proj)
    else:
        returned = plain_call(outgoing, gate_proj, up_proj, down_proj)
    placed_back = (
        (target[:, None] == jnp.arange(groups * slot_count)[None, :]) & landed[:, None]
    ).astype(jnp.bfloat16)
    routed = jnp.einsum(
        "ts,sd->td", placed_back, returned.reshape(-1, model_width), preferred_element_type=jnp.float32
    )
    return (weighting[:, None] * routed).astype(jnp.bfloat16)


def solution(mesh):
    placed = (
        P(("rep", "grp", "ing", "dp"), None),
        P(("rep", "grp", "ing", "dp"), None),
        P(("rep", "grp", "ing", "dp"), None),
        P("grp", None, ("ing", "dp")),
        P("grp", None, ("ing", "dp")),
        P("grp", ("ing", "dp"), None),
    )
    return jax.shard_map(
        on_device,
        mesh=mesh,
        in_specs=placed,
        out_specs=P(("rep", "grp", "ing", "dp"), None),
        check_vma=False,
    )
```
